512 devices in a mesh: dp: 128 (over x_lo, y, z), mp: 4 (over x_hi, core).
Axes of the slice: x: 4 (x_hi: 2, x_lo: 2; x = x_hi * 2 + x_lo), y: 4, z: 16, core: 2. Of those that a mesh axis runs over, the one named last changes fastest.
Arguments:
- image: bfloat16 [98304, 1024], P('dp', 'mp'), may hold values from -0.59765625 to 0.59765625
- text: bfloat16 [98304, 1024], P('dp', 'mp'), may hold values from -0.59765625 to 0.59765625
Outputs:
- image_grad: float32 [98304, 1024], P(('dp', 'mp'))
- text_grad: float32 [98304, 1024], P(('dp', 'mp'))
- row_loss: float32 [98304], P(('dp', 'mp'))
The draws below stay inside these ranges and needn't reach their ends.
All inputs are finite; a program needn't handle non-finite values.
Results may differ from the reference program's by a relative error of at most 0.0017.
Values may be sent and summed in bfloat16 or wider, within the bound.
A program may use at most 64 MiB of HBM per device.

```python
import jax
import jax.numpy as jnp
from jax import lax

D = 1024
ROWS = 768
TILES = 3
BATCH = 98304


def block_levels(key, dims, cuts, smallest, high):
    gain = 1.0
    for position, blocks in cuts:
        steps = jax.random.uniform(jax.random.fold_in(jax.random.fold_in(key, 6), position), (blocks,), jnp.float32, smallest / len(cuts), high / len(cuts))
        gain = gain * jnp.repeat(jnp.exp(steps), dims[position] // blocks).reshape((-1,) + (1,) * (len(dims) - 1 - position))
    return gain


def gaussian(stream_key, extent, scale, reach, split=(), kind=jnp.bfloat16):
    loudness = block_levels(stream_key, extent, split, -0.22, 0.18) if split else 1.0
    entries = jax.random.normal(stream_key, extent, jnp.float32) * scale * loudness
    return jnp.minimum(jnp.maximum(entries, -reach), reach).astype(kind)


def setup_inputs(seed: int = 0) -> dict:
    key_of = jax.random.split(jax.random.key(seed), 3)
    return {
        "image": gaussian(key_of[0], (BATCH, D), 0.1, 0.59765625, ((0, 128), (1, 4))),
        "text": gaussian(key_of[1], (BATCH, D), 0.1, 0.59765625, ((0, 128), (1, 4))),
    }


LOGIT_SCALE = 10.0
LOGIT_BIAS = -2.0


def reference(image, text):
    block_count = BATCH // ROWS
    image_blocks = image.reshape(block_count, ROWS, D)
    text_blocks = text.reshape(block_count, ROWS, D)
    row_ids = jnp.arange(ROWS, dtype=jnp.int32)
    diagonal_mask = row_ids[:, None] == row_ids[None, :]

    def per_block(text_accum, i):
        x = image_blocks[i]
        image_accum = jnp.zeros((ROWS, D), jnp.float32)
        row_total = jnp.zeros((ROWS,), jnp.float32)
        for s in range(TILES):
            b = ((i - s) % block_count).astype(jnp.int32)
            y = text_blocks[b]
            logit_tile = LOGIT_SCALE * jnp.dot(x, y.T, preferred_element_type=jnp.float32) + LOGIT_BIAS
            if s == 0:
                positive = diagonal_mask.astype(jnp.float32)
            else:
                positive = jnp.zeros((ROWS, ROWS), jnp.float32)
            label_sign = 2.0 * positive - 1.0
            row_total = row_total + jnp.sum(jax.nn.softplus(-label_sign * logit_tile), axis=1)
            coefficient = (jax.nn.sigmoid(logit_tile) - positive).astype(jnp.bfloat16)
            image_accum = image_accum + LOGIT_SCALE * jnp.dot(coefficient, y, preferred_element_type=jnp.float32)
            text_accum = text_accum.at[b].add(LOGIT_SCALE * jnp.dot(coefficient.T, x, preferred_element_type=jnp.float32))
        return text_accum, (image_accum, row_total)

    start = jnp.zeros((block_count, ROWS, D), jnp.float32)
    text_accum, (image_parts, losses) = lax.scan(per_block, start, jnp.arange(block_count, dtype=jnp.int32))
    return image_parts.reshape(BATCH, D), text_accum.reshape(BATCH, D), losses.reshape(BATCH)
```

```python
import jax
import jax.numpy as jnp
from jax import lax
from jax.sharding import PartitionSpec as P
import jax.experimental.pallas as pl
import jax.experimental.pallas.tpu as pltpu

TILES = 3
LOGIT_SCALE = 10.0
LOGIT_BIAS = -2.0
MESH = pl.DeviceIdType.MESH

GROUPS = 128
HALF = GROUPS // 2
PARTS = 4
CHUNK = 192
COLS = 256
SLOTS = TILES * PARTS


def kernel(img, txt, gi, gt, loss, xb, yb, lacc, send, recv, local):
    g, m = lax.axis_index("dp"), lax.axis_index("mp")
    sib = m + 1 - 2 * (m % 2)
    par = (m + 2) % PARTS
    base = 2 * (m // 2)
    up, down = (g + 1) % GROUPS, (g + GROUPS - 1) % GROUPS
    flows = ((img, xb, down, g % HALF == 0), (txt, yb, up, g % HALF == HALF - 1))

    def put(t, src, q, kind, slot, device, whole=False):
        dst = flows[t][1].at[q, pl.ds(slot, PARTS)] if whole else flows[t][1].at[q, slot]
        return pltpu.make_async_remote_copy(
            src_ref=src,
            dst_ref=dst,
            send_sem=send.at[t, kind, slot],
            recv_sem=recv.at[t, kind, slot],
            device_id=device,
            device_id_type=MESH,
        )

    def arrived(t, kind, slot, whole=False):
        src = flows[t][1].at[0, pl.ds(0, PARTS)] if whole else flows[t][1].at[0, 0]
        put(t, src, 0, kind, 0 if whole else slot, (g, sib), whole).wait_recv()

    own = [pltpu.make_async_copy(flows[t][0], flows[t][1].at[m, pl.ds(0, PARTS)], local.at[t]) for t in range(2)]
    for c in own:
        c.start()

    barrier = pltpu.get_barrier_semaphore()
    for device in ((g, sib), (g, par), (up, m), (down, m), (up, par), (down, par)):
        pl.semaphore_signal(barrier, inc=1, device_id=device, device_id_type=MESH)
    pl.semaphore_wait(barrier, 6)

    for k in range(PARTS):
        c = (base + 2 + k) % PARTS
        for t in range(2):
            entry, _, nxt, _ = flows[t]
            put(t, entry.at[k], m, 0, PARTS + k, (nxt, m)).start()
            put(t, entry.at[c], m, 2, c, (g, par)).start()
        if k == 0:
            for t in range(2):
                put(t, flows[t][0], m, 1, 0, (g, sib), True).start()
    gi[...] = jnp.zeros_like(gi)
    gt[...] = jnp.zeros_like(gt)
    lacc[...] = jnp.zeros_like(lacc)
    for c in own:
        c.wait()

    def slot_of(i):
        return PARTS * (i // PARTS) + (base + i) % PARTS

    def own_quarters(i):
        for e in range(2):
            o = PARTS + 2 * i + e
            for t in range(2):
                _, buf, nxt, _ = flows[t]
                arrived(t, 0, o)

                @pl.when(o < 2 * PARTS)
                def _():
                    put(t, buf.at[m, o], m, 0, o + PARTS, (nxt, m)).start()

                put(t, buf.at[m, o], m, 1, o, (g, sib)).start()

    def partner_quarters(i):
        slot = slot_of(i)
        for t in range(2):
            _, buf, nxt, across = flows[t]
            arrived(t, 2, slot)

            @pl.when(i < 2 * PARTS)
            def _():
                q = jnp.where(across, m, par)
                to = jnp.where(across, par, m)
                there = PARTS * (i // PARTS) + (2 * (to // 2) + i) % PARTS
                put(t, buf.at[q, there], q, 2, there + PARTS, (nxt, to)).start()

            put(t, buf.at[par, slot], par, 3, slot, (g, sib)).start()

    def tile(t, slot):
        mine, other, out = (xb, yb, gi) if t == 1 else (yb, xb, gt)
        acc = None
        for q in range(PARTS):
            d = lax.dot_general(
                mine[q, m], other[q, slot], (((1,), (1,)), ((), ())), preferred_element_type=jnp.float32
            )
            acc = d if acc is None else acc + d
        logit = LOGIT_SCALE * acc + LOGIT_BIAS
        rows = lax.broadcasted_iota(jnp.int32, (CHUNK, CHUNK), 0)
        cols = lax.broadcasted_iota(jnp.int32, (CHUNK, CHUNK), 1)
        positive = (rows - cols) == jnp.where(slot == m, 0, 4 * CHUNK)
        if t == 1:
            x = jnp.where(positive, -logit, logit)
            lacc[...] += jnp.maximum(x, 0.0) + jnp.log1p(jnp.exp(-jnp.abs(x)))
        coefficient = 1.0 / (1.0 + jnp.exp(-logit)) - jnp.where(positive, 1.0, 0.0)
        coefficient = coefficient.astype(jnp.bfloat16)
        for q in range(PARTS):
            out[:, pl.ds(q * COLS, COLS)] += jnp.dot(coefficient, other[q, slot], preferred_element_type=jnp.float32)

    def tiles(i):
        slot = slot_of(i)
        for t in (1, 0):
            tile(t, slot)

    def from_core(i):
        slot = slot_of(i)
        for t in range(2):
            arrived(t, 3, slot)

            @pl.when(i >= PARTS)
            def _():
                arrived(t, 1, slot)

    own_quarters(0)
    partner_quarters(0)
    own_quarters(1)
    partner_quarters(1)
    for t in range(2):
        arrived(t, 1, 0, True)
    from_core(0)
    from_core(1)

    @pl.loop(1, SLOTS + 1)
    def _(i):
        @pl.when((i >= 2) & (i < 4))
        def _():
            own_quarters(i)

        @pl.when((i >= 2) & (i < SLOTS))
        def _():
            partner_quarters(i)

        @pl.when(i >= 3)
        def _():
            from_core(i - 1)

        tiles(i - 1)

    gi[...] *= LOGIT_SCALE
    gt[...] *= LOGIT_SCALE
    loss[...] = jnp.sum(jnp.transpose(lacc[...]), axis=0, keepdims=True)

    for t in range(2):
        put(t, flows[t][0], m, 1, 0, (g, sib), True).wait_send()

        @pl.loop(0, SLOTS)
        def _(slot):
            for kind in range(PARTS):
                def done():
                    put(t, flows[t][1].at[0, 0], 0, kind, slot, (g, sib)).wait_send()

                if kind < 2:
                    pl.when(slot >= PARTS)(done)
                else:
                    done()


def local(image, text):
    rows, cols = image.shape
    width = cols * PARTS
    block = (PARTS, rows // PARTS, cols)
    flops = 2 * 4 * TILES * CHUNK * rows * width
    gi, gt, loss = pl.pallas_call(
        kernel,
        out_shape=(
            jax.ShapeDtypeStruct((CHUNK, width), jnp.float32),
            jax.ShapeDtypeStruct((CHUNK, width), jnp.float32),
            jax.ShapeDtypeStruct((1, CHUNK), jnp.float32),
        ),
        in_specs=[pl.BlockSpec(memory_space=pl.ANY)] * 2,
        out_specs=[pl.BlockSpec(memory_space=pltpu.VMEM)] * 3,
        scratch_shapes=[
            pltpu.VMEM((PARTS, SLOTS, CHUNK, COLS), jnp.bfloat16),
            pltpu.VMEM((PARTS, SLOTS, CHUNK, COLS), jnp.bfloat16),
            pltpu.VMEM((CHUNK, CHUNK), jnp.float32),
            pltpu.SemaphoreType.DMA((2, PARTS, SLOTS)),
            pltpu.SemaphoreType.DMA((2, PARTS, SLOTS)),
            pltpu.SemaphoreType.DMA((2,)),
        ],
        compiler_params=pltpu.CompilerParams(
            collective_id=0, has_side_effects=True, vmem_limit_bytes=40 * 1024 * 1024
        ),
        cost_estimate=pl.CostEstimate(
            flops=flops, bytes_accessed=4 * rows * cols * 2, transcendentals=4 * TILES * CHUNK * rows
        ),
    )(image.reshape(block), text.reshape(block))
    return gi, gt, loss.reshape(CHUNK)


def solution(mesh):
    in_specs = (P("dp", "mp"), P("dp", "mp"))
    out_specs = (P(("dp", "mp"), None), P(("dp", "mp"), None), P(("dp", "mp")))
    return jax.shard_map(local, mesh=mesh, in_specs=in_specs, out_specs=out_specs, check_vma=False)
```

```python
import jax
import jax.numpy as jnp
from jax import lax
from jax.sharding import PartitionSpec as P
import jax.experimental.pallas as pl
import jax.experimental.pallas.tpu as pltpu

TILES = 3
LOGIT_SCALE = 10.0
LOGIT_BIAS = -2.0
MESH = pl.DeviceIdType.MESH

GROUPS = 128
HALF = GROUPS // 2
PARTS = 4
CHUNK = 192
COLS = 256
X_AHEAD = 2
GATES = (8, 7)
LATE = 9
SHIFT = 4
ALONG = 16
STEPS = 21
SLOTS = TILES * PARTS


def kernel(img, txt, gi, gt, loss, held, grads, lacc, send, recv, local):
    g, m = lax.axis_index("dp"), lax.axis_index("mp")
    sib = m + 1 - 2 * (m % 2)
    par = (m + 2) % PARTS
    base = 2 * (m // 2)
    up, down = (g + 1) % GROUPS, (g + GROUPS - 1) % GROUPS
    z = g % ALONG
    flows = (
        (img, held.at[0], down, g % HALF == 0, g % HALF == HALF - 1, g % HALF == HALF - 2),
        (txt, held.at[1], up, g % HALF == HALF - 1, g % HALF == 0, g % HALF == 1),
    )

    def put(t, src, q, kind, slot, device, whole=False, sem=None):
        dst = flows[t][1].at[q, pl.ds(slot, PARTS)] if whole else flows[t][1].at[q, slot]
        return pltpu.make_async_remote_copy(
            src_ref=src,
            dst_ref=dst,
            send_sem=send.at[t, kind if sem is None else sem, slot],
            recv_sem=recv.at[t, kind, slot],
            device_id=device,
            device_id_type=MESH,
        )

    def arrived(t, kind, slot, whole=False):
        ref = held.at[t, 0, pl.ds(0, PARTS)] if whole else held.at[t, 0, 0]
        pltpu.make_async_remote_copy(
            src_ref=ref,
            dst_ref=ref,
            send_sem=send.at[t, kind, slot],
            recv_sem=recv.at[t, kind, slot],
            device_id=(g, sib),
            device_id_type=MESH,
        ).wait_recv()

    own = [pltpu.make_async_copy(flows[t][0], flows[t][1].at[m, pl.ds(0, PARTS)], local.at[t]) for t in range(2)]
    for c in own:
        c.start()

    barrier = pltpu.get_barrier_semaphore()
    for device in ((g, sib), (g, par), (up, m), (down, m), (up, par), (down, par)):
        pl.semaphore_signal(barrier, inc=1, device_id=device, device_id_type=MESH)
    pl.semaphore_wait(barrier, 6)

    def onward(t, kind, slot):
        _, buf, nxt, *_ = flows[t]
        q = jnp.where(kind == 0, m, par)
        put(t, buf.at[q, slot - PARTS], q, kind, slot, (nxt, m)).start()

    def to_partner(j):
        c = (base + 2 + j) % PARTS
        for t in range(2):
            put(t, flows[t][0].at[c], m, 2, c, (g, par)).start()

    for k in range(PARTS):
        for t in range(2):
            entry, _, nxt, across, *_ = flows[t]
            pl.when(jnp.logical_not(across))(put(t, entry.at[k], m, 0, PARTS + k, (nxt, m)).start)
        if k < X_AHEAD:
            to_partner(k)
        if k == 0:
            for t in range(2):
                put(t, flows[t][0], m, 1, 0, (g, sib), True).start()
    grads[...] = jnp.zeros_like(grads)
    lacc[...] = jnp.zeros_like(lacc)
    for c in own:
        c.wait()

    def chunk_of(t, i):
        _, _, _, _, late, second = flows[t]
        absolute = ((i >= PARTS) & late) | ((i >= 2 * PARTS) & second)
        return PARTS * (i // PARTS) + (jnp.where(absolute, 0, base) + i) % PARTS

    def over_x(j):
        pl.when(j < PARTS - X_AHEAD)(lambda: to_partner(j + X_AHEAD))
        c = (base + j) % PARTS
        for t in range(2):
            _, buf, _, across, _, _ = flows[t]
            arrived(t, 2, c)
            pl.when(jnp.logical_not(across))(lambda: onward(t, 2, c + PARTS))
            put(t, buf.at[par, c], par, 3, c, (g, sib)).start()

    def shifts(t):
        if t == 0:
            return 0, 0
        return jnp.where(z == 0, SHIFT, 0), jnp.where(z <= 1, SHIFT, 0)

    def arrivals(n, t):
        _, buf, nxt, across, late, second = flows[t]
        normal = jnp.logical_not(late | second)
        n1, n2 = n - shifts(t)[0], n - shifts(t)[1]
        slot = jnp.where((n1 >= 0) & (n1 < 4) & jnp.logical_not(late), 4 + n1, -1)
        slot = jnp.where(normal & (n2 >= 5) & (n2 < 12) & (n2 % 2 == 1), 8 + (n2 - 5) // 2, slot)
        slot = jnp.where(second & (n >= LATE + 2) & (n < LATE + 6), n - LATE + 6, slot)
        slot = jnp.where(late & (n >= LATE) & (n < LATE + 8), n - LATE + 4, slot)

        @pl.when(slot >= 0)
        def _():
            arrived(t, 0, slot)

            @pl.when(late)
            def _():
                put(t, buf.at[m, slot], m, 2, slot, (g, par), sem=PARTS).start()
                pl.when(slot < 2 * PARTS)(lambda: onward(t, 0, slot + PARTS))

            put(t, buf.at[m, slot], m, 1, slot, (g, sib)).start()

        i = jnp.where(jnp.logical_not(late) & (n1 >= 4) & (n1 < 12) & (n1 % 2 == 0), 4 + (n1 - 4) // 2, -1)
        i = jnp.where(normal & (n2 >= 12) & (n2 < 16), n2 - 4, i)
        i = jnp.where(second & (n >= LATE + 4) & (n < LATE + 8), n - LATE + 4, i)
        i = jnp.where(late & (n >= LATE + 2) & (n < LATE + 10), n - LATE + 2, i)

        @pl.when(i >= 0)
        def _():
            half = chunk_of(t, i)
            arrived(t, 2, half)
            pl.when(late & (half < 2 * PARTS))(lambda: onward(t, 2, half + PARTS))
            put(t, buf.at[par, half], par, 3, half, (g, sib)).start()

    def sends(n, t):
        _, _, _, across, late, _ = flows[t]
        normal = jnp.logical_not(across | late)
        n1 = n - shifts(t)[0]

        @pl.when(normal & (n1 >= 0) & (n1 < 8) & (n1 % 2 == 1))
        def _():
            onward(t, 0, 2 * PARTS + n1 // 2)

        @pl.when(normal & (n1 >= 8) & (n1 < 12))
        def _():
            onward(t, 2, chunk_of(t, n1 - 4) + PARTS)

        gate = GATES[t]

        @pl.when(across & (n >= gate) & (n <= gate + 5))
        def _():
            @pl.when(n == gate)
            def _():
                for k in range(3):
                    onward(t, 0, PARTS + k)

            pl.when(n > gate)(lambda: onward(t, 0, n - gate + 2 + PARTS))

    def tile(t, slot):
        def rows_of(q):
            return held[t, q, pl.ds(slot, 2)].reshape(2 * CHUNK, COLS)

        acc = None
        for q in range(PARTS):
            d = lax.dot_general(
                held[1 - t, q, m], rows_of(q), (((1,), (1,)), ((), ())), preferred_element_type=jnp.float32
            )
            acc = d if acc is None else acc + d
        logit = LOGIT_SCALE * acc + LOGIT_BIAS
        rows = lax.broadcasted_iota(jnp.int32, acc.shape, 0)
        cols = lax.broadcasted_iota(jnp.int32, acc.shape, 1)
        positive = (cols - rows) == jnp.where(slot < PARTS, (m - slot) * CHUNK, 4 * CHUNK)
        @pl.when(t == 1)
        def _():
            x = jnp.where(positive, -logit, logit)
            lacc[...] += jnp.maximum(x, 0.0) + jnp.log1p(jnp.exp(-jnp.abs(x)))
        coefficient = 1.0 / (1.0 + jnp.exp(-logit)) - jnp.where(positive, 1.0, 0.0)
        coefficient = coefficient.astype(jnp.bfloat16)
        for q in range(PARTS):
            grads[t, :, pl.ds(q * COLS, COLS)] += jnp.dot(coefficient, rows_of(q), preferred_element_type=jnp.float32)

    def reached(n, t):
        _, _, _, _, late, second = flows[t]
        n1, n2 = n - shifts(t)[0], n - shifts(t)[1]
        own_block = jnp.where(n < 8, jnp.clip(n - 3, 0, 3), PARTS)
        farther = jnp.where(second, n - LATE + 4, n2 - 4)
        chunks = jnp.maximum(jnp.maximum(own_block, jnp.minimum(n1 - 4, 2 * PARTS)), farther)
        chunks = jnp.where(late, jnp.maximum(own_block, n - LATE + 2), chunks)
        return jnp.minimum(chunks, SLOTS) // 2

    apart = flows[0][4] | flows[1][4] | flows[0][5] | flows[1][5] | (z <= 1)
    steps = jnp.where(apart, STEPS, STEPS - 4)

    @pl.loop(0, steps)
    def _(n):
        pl.when((n < 2 * PARTS) & (n % 2 == 1))(lambda: over_x(n // 2))
        for t in range(2):
            arrivals(n, t)
        for t in range(2):
            sends(n, t)

        @pl.when(n == 4)
        def _():
            for t in range(2):
                arrived(t, 1, 0, True)
                arrived(t, 3, base)
                arrived(t, 3, base + 1)

        def either(t, of):
            return jnp.where(t == 1, of(1), of(0))

        @pl.loop(0, 2)
        def _(k):
            t = 1 - k

            @pl.loop(either(t, lambda t: reached(n - 1, t)), either(t, lambda t: reached(n, t)))
            def _(i):
                slot = either(t, lambda t: chunk_of(t, 2 * i))
                for k in range(2):
                    pl.when(i >= PARTS // 2)(lambda: arrived(t, 1, slot + k))
                    pl.when(i >= 1)(lambda: arrived(t, 3, slot + k))
                tile(t, slot)

    gi[...] = grads[1] * LOGIT_SCALE
    gt[...] = grads[0] * LOGIT_SCALE
    loss[...] = jnp.sum(jnp.transpose(lacc[...]), axis=0, keepdims=True)

    for t in range(2):
        put(t, flows[t][0], m, 1, 0, (g, sib), True).wait_send()

        @pl.loop(0, SLOTS)
        def _(slot):
            def done(kind):
                put(t, flows[t][1].at[0, 0], 0, kind, slot, (g, sib)).wait_send()

            done(3)
            pl.when((slot < PARTS) | jnp.logical_not(flows[t][3]))(lambda: done(2))

            @pl.when(slot >= PARTS)
            def _():
                done(0)
                done(1)
                pl.when(flows[t][4])(lambda: done(PARTS))


def local(image, text):
    rows, cols = image.shape
    width = cols * PARTS
    block = (PARTS, rows // PARTS, cols)
    flops = 2 * 4 * TILES * CHUNK * rows * width
    gi, gt, loss = pl.pallas_call(
        kernel,
        out_shape=(
            jax.ShapeDtypeStruct((CHUNK, width), jnp.float32),
            jax.ShapeDtypeStruct((CHUNK, width), jnp.float32),
            jax.ShapeDtypeStruct((1, CHUNK), jnp.float32),
        ),
        in_specs=[pl.BlockSpec(memory_space=pl.ANY)] * 2,
        out_specs=[pl.BlockSpec(memory_space=pltpu.VMEM)] * 3,
        scratch_shapes=[
            pltpu.VMEM((2, PARTS, SLOTS, CHUNK, COLS), jnp.bfloat16),
            pltpu.VMEM((2, CHUNK, width), jnp.float32),
            pltpu.VMEM((CHUNK, 2 * CHUNK), jnp.float32),
            pltpu.SemaphoreType.DMA((2, PARTS + 1, SLOTS)),
            pltpu.SemaphoreType.DMA((2, PARTS, SLOTS)),
            pltpu.SemaphoreType.DMA((2,)),
        ],
        compiler_params=pltpu.CompilerParams(
            collective_id=0, has_side_effects=True, vmem_limit_bytes=40 * 1024 * 1024
        ),
        cost_estimate=pl.CostEstimate(
            flops=flops, bytes_accessed=4 * rows * cols * 2, transcendentals=4 * TILES * CHUNK * rows
        ),
    )(image.reshape(block), text.reshape(block))
    return gi, gt, loss.reshape(CHUNK)


def solution(mesh):
    in_specs = (P("dp", "mp"), P("dp", "mp"))
    out_specs = (P(("dp", "mp"), None), P(("dp", "mp"), None), P(("dp", "mp")))
    return jax.shard_map(local, mesh=mesh, in_specs=in_specs, out_specs=out_specs, check_vma=False)
```

```python
import jax
import jax.numpy as jnp
from jax import lax
from jax.sharding import PartitionSpec as P
import jax.experimental.pallas as pl
import jax.experimental.pallas.tpu as pltpu

TILES = 3
LOGIT_SCALE = 10.0
LOGIT_BIAS = -2.0
MESH = pl.DeviceIdType.MESH

GROUPS = 128
HALF = GROUPS // 2
PARTS = 4
CHUNK = 192
COLS = 256
X_AHEAD = 2
GATES = (7, 7)
LATE = 9
SHIFT = 4
ALONG = 16
STEPS = 21
SLOTS = TILES * PARTS


def kernel(img, txt, gi, gt, loss, held, grads, lacc, send, recv, local):
    g, m = lax.axis_index("dp"), lax.axis_index("mp")
    sib = m + 1 - 2 * (m % 2)
    par = (m + 2) % PARTS
    base = 2 * (m // 2)
    up, down = (g + 1) % GROUPS, (g + GROUPS - 1) % GROUPS
    z = g % ALONG
    flows = (
        (img, held.at[0], down, g % HALF == 0, g % HALF == HALF - 1, g % HALF == HALF - 2),
        (txt, held.at[1], up, g % HALF == HALF - 1, g % HALF == 0, g % HALF == 1),
    )

    def put(t, src, q, kind, slot, device, whole=False, sem=None):
        dst = flows[t][1].at[q, pl.ds(slot, PARTS)] if whole else flows[t][1].at[q, slot]
        return pltpu.make_async_remote_copy(
            src_ref=src,
            dst_ref=dst,
            send_sem=send.at[t, kind if sem is None else sem, slot],
            recv_sem=recv.at[t, kind, slot],
            device_id=device,
            device_id_type=MESH,
        )

    def arrived(t, kind, slot, whole=False):
        ref = held.at[t, 0, pl.ds(0, PARTS)] if whole else held.at[t, 0, 0]
        pltpu.make_async_remote_copy(
            src_ref=ref,
            dst_ref=ref,
            send_sem=send.at[t, kind, slot],
            recv_sem=recv.at[t, kind, slot],
            device_id=(g, sib),
            device_id_type=MESH,
        ).wait_recv()

    own = [pltpu.make_async_copy(flows[t][0], flows[t][1].at[m, pl.ds(0, PARTS)], local.at[t]) for t in range(2)]
    for c in own:
        c.start()

    barrier = pltpu.get_barrier_semaphore()
    for device in ((g, sib), (g, par), (up, m), (down, m), (up, par), (down, par)):
        pl.semaphore_signal(barrier, inc=1, device_id=device, device_id_type=MESH)
    pl.semaphore_wait(barrier, 6)

    def onward(t, kind, slot):
        _, buf, nxt, *_ = flows[t]
        q = jnp.where(kind == 0, m, par)
        put(t, buf.at[q, slot - PARTS], q, kind, slot, (nxt, m)).start()

    def to_partner(j):
        c = (base + 2 + j) % PARTS
        for t in range(2):
            put(t, flows[t][0].at[c], m, 2, c, (g, par)).start()

    for k in range(PARTS):
        for t in range(2):
            entry, _, nxt, across, *_ = flows[t]
            pl.when(jnp.logical_not(across))(put(t, entry.at[k], m, 0, PARTS + k, (nxt, m)).start)
        if k < X_AHEAD:
            to_partner(k)
        if k == 0:
            for t in range(2):
                put(t, flows[t][0], m, 1, 0, (g, sib), True).start()
    grads[...] = jnp.zeros_like(grads)
    lacc[...] = jnp.zeros_like(lacc)
    for c in own:
        c.wait()

    def chunk_of(t, i):
        _, _, _, _, late, second = flows[t]
        absolute = ((i >= PARTS) & late) | ((i >= 2 * PARTS) & second)
        return PARTS * (i // PARTS) + (jnp.where(absolute, 0, base) + i) % PARTS

    def over_x(j):
        pl.when(j < PARTS - X_AHEAD)(lambda: to_partner(j + X_AHEAD))
        c = (base + j) % PARTS
        for t in range(2):
            _, buf, _, across, _, _ = flows[t]
            arrived(t, 2, c)
            pl.when(jnp.logical_not(across))(lambda: onward(t, 2, c + PARTS))
            put(t, buf.at[par, c], par, 3, c, (g, sib)).start()

    def shifts(t):
        if t == 0:
            return 0, 0
        return jnp.where(z == 0, SHIFT, 0), jnp.where(z <= 1, SHIFT, 0)

    def arrivals(n, t):
        _, buf, nxt, across, late, second = flows[t]
        normal = jnp.logical_not(late | second)
        n1, n2 = n - shifts(t)[0], n - shifts(t)[1]
        slot = jnp.where((n1 >= 0) & (n1 < 4) & jnp.logical_not(late), 4 + n1, -1)
        slot = jnp.where(normal & (n2 >= 5) & (n2 < 12) & (n2 % 2 == 1), 8 + (n2 - 5) // 2, slot)
        slot = jnp.where(second & (n >= LATE + 2) & (n < LATE + 6), n - LATE + 6, slot)
        slot = jnp.where(late & (n >= LATE) & (n < LATE + 8), n - LATE + 4, slot)

        @pl.when(slot >= 0)
        def _():
            arrived(t, 0, slot)

            @pl.when(late)
            def _():
                put(t, buf.at[m, slot], m, 2, slot, (g, par), sem=PARTS).start()
                pl.when(slot < 2 * PARTS)(lambda: onward(t, 0, slot + PARTS))

            put(t, buf.at[m, slot], m, 1, slot, (g, sib)).start()

        i = jnp.where(jnp.logical_not(late) & (n1 >= 4) & (n1 < 12) & (n1 % 2 == 0), 4 + (n1 - 4) // 2, -1)
        i = jnp.where(normal & (n2 >= 12) & (n2 < 16), n2 - 4, i)
        i = jnp.where(second & (n >= LATE + 6) & (n < LATE + 10), n - LATE + 2, i)
        i = jnp.where(late & (n >= LATE + 4) & (n < LATE + 12), n - LATE + 0, i)

        @pl.when(i >= 0)
        def _():
            half = chunk_of(t, i)
            arrived(t, 2, half)
            pl.when(late & (half < 2 * PARTS))(lambda: onward(t, 2, half + PARTS))
            put(t, buf.at[par, half], par, 3, half, (g, sib)).start()

    def sends(n, t):
        _, _, _, across, late, _ = flows[t]
        normal = jnp.logical_not(across | late)
        n1 = n - shifts(t)[0]

        @pl.when(normal & (n1 >= 0) & (n1 < 8) & (n1 % 2 == 1))
        def _():
            onward(t, 0, 2 * PARTS + n1 // 2)

        @pl.when(normal & (n1 >= 8) & (n1 < 12))
        def _():
            onward(t, 2, chunk_of(t, n1 - 4) + PARTS)

    def sends_over_x(n, t):
        across = flows[t][3]
        gate = GATES[t]

        @pl.when(across & (n >= gate) & (n <= gate))
        def _():
            @pl.when(n == gate)
            def _():
                for k in range(2 * PARTS):
                    onward(t, 0, PARTS + k)

    def tile(t, slot):
        def rows_of(q):
            return held[t, q, pl.ds(slot, 2)].reshape(2 * CHUNK, COLS)

        acc = None
        for q in range(PARTS):
            d = lax.dot_general(
                held[1 - t, q, m], rows_of(q), (((1,), (1,)), ((), ())), preferred_element_type=jnp.float32
            )
            acc = d if acc is None else acc + d
        logit = LOGIT_SCALE * acc + LOGIT_BIAS
        rows = lax.broadcasted_iota(jnp.int32, acc.shape, 0)
        cols = lax.broadcasted_iota(jnp.int32, acc.shape, 1)
        positive = (cols - rows) == jnp.where(slot < PARTS, (m - slot) * CHUNK, 4 * CHUNK)
        @pl.when(t == 1)
        def _():
            x = jnp.where(positive, -logit, logit)
            lacc[...] += jnp.maximum(x, 0.0) + jnp.log1p(jnp.exp(-jnp.abs(x)))
        coefficient = 1.0 / (1.0 + jnp.exp(-logit)) - jnp.where(positive, 1.0, 0.0)
        coefficient = coefficient.astype(jnp.bfloat16)
        for q in range(PARTS):
            grads[t, :, pl.ds(q * COLS, COLS)] += jnp.dot(coefficient, rows_of(q), preferred_element_type=jnp.float32)

    def reached(n, t):
        _, _, _, _, late, second = flows[t]
        n1, n2 = n - shifts(t)[0], n - shifts(t)[1]
        own_block = jnp.where(n < 8, jnp.clip(n - 3, 0, 3), PARTS)
        farther = jnp.where(second, n - LATE + 2, n2 - 4)
        chunks = jnp.maximum(jnp.maximum(own_block, jnp.minimum(n1 - 4, 2 * PARTS)), farther)
        chunks = jnp.where(late, jnp.maximum(own_block, n - LATE + 0), chunks)
        return jnp.minimum(chunks, SLOTS) // 2

    late, second = flows[0][4] | flows[1][4], flows[0][5] | flows[1][5]
    steps = jnp.where(late, LATE + 13, jnp.where(second, LATE + 11, jnp.where(z <= 1, STEPS, STEPS - 4)))

    @pl.loop(0, steps)
    def _(n):
        pl.when((n < 2 * PARTS) & (n % 2 == 1))(lambda: over_x(n // 2))
        for t in (1, 0):
            sends_over_x(n, t)
        for t in range(2):
            arrivals(n, t)
        for t in range(2):
            sends(n, t)

        @pl.when(n == 4)
        def _():
            for t in range(2):
                arrived(t, 1, 0, True)
                arrived(t, 3, base)
                arrived(t, 3, base + 1)

        def either(t, of):
            return jnp.where(t == 1, of(1), of(0))

        @pl.loop(0, 2)
        def _(k):
            t = 1 - k

            @pl.loop(either(t, lambda t: reached(n - 1, t)), either(t, lambda t: reached(n, t)))
            def _(i):
                slot = either(t, lambda t: chunk_of(t, 2 * i))
                for k in range(2):
                    pl.when(i >= PARTS // 2)(lambda: arrived(t, 1, slot + k))
                    pl.when(i >= 1)(lambda: arrived(t, 3, slot + k))
                tile(t, slot)

    gi[...] = grads[1] * LOGIT_SCALE
    gt[...] = grads[0] * LOGIT_SCALE
    loss[...] = jnp.sum(jnp.transpose(lacc[...]), axis=0, keepdims=True)

    for t in range(2):
        put(t, flows[t][0], m, 1, 0, (g, sib), True).wait_send()

        @pl.loop(0, SLOTS)
        def _(slot):
            def done(kind):
                put(t, flows[t][1].at[0, 0], 0, kind, slot, (g, sib)).wait_send()

            done(3)
            pl.when((slot < PARTS) | jnp.logical_not(flows[t][3]))(lambda: done(2))

            @pl.when(slot >= PARTS)
            def _():
                done(0)
                done(1)
                pl.when(flows[t][4])(lambda: done(PARTS))


def local(image, text):
    rows, cols = image.shape
    width = cols * PARTS
    block = (PARTS, rows // PARTS, cols)
    flops = 2 * 4 * TILES * CHUNK * rows * width
    gi, gt, loss = pl.pallas_call(
        kernel,
        out_shape=(
            jax.ShapeDtypeStruct((CHUNK, width), jnp.float32),
            jax.ShapeDtypeStruct((CHUNK, width), jnp.float32),
            jax.ShapeDtypeStruct((1, CHUNK), jnp.float32),
        ),
        in_specs=[pl.BlockSpec(memory_space=pl.ANY)] * 2,
        out_specs=[pl.BlockSpec(memory_space=pltpu.VMEM)] * 3,
        scratch_shapes=[
            pltpu.VMEM((2, PARTS, SLOTS, CHUNK, COLS), jnp.bfloat16),
            pltpu.VMEM((2, CHUNK, width), jnp.float32),
            pltpu.VMEM((CHUNK, 2 * CHUNK), jnp.float32),
            pltpu.SemaphoreType.DMA((2, PARTS + 1, SLOTS)),
            pltpu.SemaphoreType.DMA((2, PARTS, SLOTS)),
            pltpu.SemaphoreType.DMA((2,)),
        ],
        compiler_params=pltpu.CompilerParams(
            collective_id=0, has_side_effects=True, vmem_limit_bytes=40 * 1024 * 1024
        ),
        cost_estimate=pl.CostEstimate(
            flops=flops, bytes_accessed=4 * rows * cols * 2, transcendentals=4 * TILES * CHUNK * rows
        ),
    )(image.reshape(block), text.reshape(block))
    return gi, gt, loss.reshape(CHUNK)


def solution(mesh):
    in_specs = (P("dp", "mp"), P("dp", "mp"))
    out_specs = (P(("dp", "mp"), None), P(("dp", "mp"), None), P(("dp", "mp")))
    return jax.shard_map(local, mesh=mesh, in_specs=in_specs, out_specs=out_specs, check_vma=False)
```
